32 devices in a mesh: slab: 2 (over y), row: 8 (over z, x), col: 2 (over core).
Axes of the slice: x: 2, y: 2, z: 4, core: 2. Of those that a mesh axis runs over, the one named last changes fastest.
Arguments:
- start: float32 [1024, 4096], P(('slab', 'row'), 'col'), parts along dimension 0, may hold values from -5 to 6
- dest_tile: int32 [262144], P(('slab', 'row', 'col')), parts along dimension 0, may hold values from 0 to 15, as said below
- cell_row: int32 [262144], P(('slab', 'row', 'col')), parts along dimension 0, may hold values from 0 to 63
- cell_col: int32 [262144], P(('slab', 'row', 'col')), parts along dimension 0, may hold values from 0 to 2047
- source_type: int32 [262144], P(('slab', 'row', 'col')), parts along dimension 0, may hold values from 0 to 2
- sounding_value: float32 [262144], P(('slab', 'row', 'col')), parts along dimension 0, may hold values from -6 to 6
- sounding_weight: float32 [262144], P(('slab', 'row', 'col')), parts along dimension 0, may hold values from 0.1 to 10
- type_gain: float32 [3], replicated, may hold values from 0.3 to 3
Outputs:
- surface: float32 [1024, 4096], P(('slab', 'row'), 'col'), parts along dimension 0
The draws below stay inside these ranges and needn't reach their ends.
There are 2 independent parts, one for each index of `slab`. The reference program is written for one: setup_inputs(seed, part) draws one part's arguments, and reference() takes and returns one part's arrays. A program takes and returns all parts, laid end to end along the dimension named above; an argument that names none is the same for every part. Nothing has to cross between parts.
Inputs may be any that keep to these rules, and one draw needn't show every extreme that they name: `dest_tile`: each track owner sends at most 640 soundings to any one tile, and in every draw some tile receives exactly 640 from every track owner.
All inputs are finite; a program needn't handle non-finite values.
Results may differ from the reference program's by a relative error of at most 0.0003.
Values sent between devices are 32-bit elements; how exact they have to be, the bound alone decides.
A program may use at most 64 MiB of HBM per device.

```python
import math
import jax
import jax.numpy as jnp

TR = 64
TC = 2048
SND_DEV = 8192
SWEEPS = 4
TYPES = 3
TILES = 16
CAP = 640
NR = 512
NC = 4096
SOUNDINGS = 131072
N_COL = 2


def draw_start(key, part):
    key = jax.random.fold_in(key, 5)
    rough = jax.random.truncated_normal(key, -5.0, 5.0, (NR, NC), jnp.float32)
    return rough


def draw_dest_tile(key, part):
    key = jax.random.fold_in(key, 11)
    key_busy, key_blocks = jax.random.split(key)
    busiest = jax.random.randint(key_busy, (), 0, TILES, jnp.int32)
    candidates = jnp.arange((TILES - 1) * CAP, dtype=jnp.int32) // CAP

    def one_block(block_key):
        first_key, second_key = jax.random.split(block_key)
        chosen = jax.random.permutation(first_key, candidates)[:SND_DEV - CAP]
        chosen = chosen + (chosen >= busiest).astype(jnp.int32)
        assigned = jnp.concatenate([jnp.full((CAP,), busiest, jnp.int32), chosen])
        return jax.random.permutation(second_key, assigned)
    blocks = jax.vmap(one_block)(jax.random.split(key_blocks, TILES))
    return blocks.reshape(-1)


def place_ends(values, rng, smallest, top_value):
    index_at = [jax.random.randint(jax.random.fold_in(rng, axis), (), 0, length) for axis, length in enumerate(values.shape)]
    longest = values.shape.index(max(values.shape))
    next_to = index_at[:longest] + [(index_at[longest] + 1) % values.shape[longest]] + index_at[longest + 1:]
    return values.at[tuple(index_at)].set(smallest).at[tuple(next_to)].set(top_value)


def level_of(rng, extent, cuts, smallest, high):
    factor_of = 1.0
    for axis_at, shards_of in cuts:
        draws = jax.random.uniform(jax.random.fold_in(jax.random.fold_in(rng, 6), axis_at), (shards_of,), jnp.float32, smallest / len(cuts), high / len(cuts))
        factor_of = factor_of * jnp.repeat(jnp.exp(draws), extent[axis_at] // shards_of).reshape((-1,) + (1,) * (len(extent) - 1 - axis_at))
    return factor_of


def normal_values(own_key, dims, spread, limit, cuts=(), held_as=jnp.bfloat16):
    gain = level_of(own_key, dims, cuts, -0.22, 0.18) if cuts else 1.0
    drawn = jax.random.normal(own_key, dims, jnp.float32) * spread * gain
    return jnp.minimum(jnp.maximum(drawn, -limit), limit).astype(held_as)


def setup_inputs(seed: int = 0, part: int = 0) -> dict:
    splits = jax.random.split(jax.random.key(seed), 9)
    own_keys = jax.random.split(jax.random.fold_in(splits[8], part), 9)
    start = draw_start(jax.random.fold_in(jax.random.fold_in(splits[8], part), 71), part)
    dest_tile = draw_dest_tile(jax.random.fold_in(jax.random.fold_in(splits[8], part), 71), part)
    cell_row = place_ends(jax.random.randint(own_keys[2], (SOUNDINGS,), 0, TR), jax.random.fold_in(own_keys[2], 1), 0, TR - 1).astype(jnp.int32)
    cell_col = place_ends(jax.random.randint(own_keys[3], (SOUNDINGS,), 0, TC), jax.random.fold_in(own_keys[3], 1), 0, TC - 1).astype(jnp.int32)
    source_type = place_ends(jax.random.randint(own_keys[4], (SOUNDINGS,), 0, TYPES), jax.random.fold_in(own_keys[4], 1), 0, TYPES - 1).astype(jnp.int32)
    sounding_value = normal_values(own_keys[5], (SOUNDINGS,), 1.0, 6.0, ((0, 16),), jnp.float32)
    sounding_weight = jnp.clip(jnp.exp(math.log(10.0) - 4.6051702 * jax.random.uniform(own_keys[6], (SOUNDINGS,), jnp.float32) ** level_of(own_keys[6], (SOUNDINGS,), ((0, 16),), -0.2, 0.2)), 0.1, 10.0)
    type_gain = jnp.clip(jnp.exp(jax.random.uniform(splits[7], (TYPES,), jnp.float32, math.log(0.3), math.log(3.0))), 0.3, 3.0)
    return dict(start=start, dest_tile=dest_tile, cell_row=cell_row, cell_col=cell_col, source_type=source_type, sounding_value=sounding_value, sounding_weight=sounding_weight, type_gain=type_gain)


tension = 0.35
centre_weight = 20.0 * (1.0 - tension) + 4.0 * tension
near_weight = 8.0 * (1.0 - tension) + tension
corner_weight = 2.0 * (1.0 - tension)
distant_weight = 1.0 - tension
damping = 0.5


def neighbour_sums(padded):
    height = padded.shape[0] - 4
    width = padded.shape[1] - 4

    def shifted(down, across):
        return padded[2 + down:2 + down + height, 2 + across:2 + across + width]

    centre = shifted(0, 0)
    near = shifted(1, 0) + shifted(-1, 0) + shifted(0, 1) + shifted(0, -1)
    corner = shifted(1, 1) + shifted(1, -1) + shifted(-1, 1) + shifted(-1, -1)
    distant = shifted(2, 0) + shifted(-2, 0) + shifted(0, 2) + shifted(0, -2)
    return centre, near, corner, distant


def relax_step(padded, data_weight, data_moment):
    centre, near, corner, distant = neighbour_sums(padded)
    applied = centre_weight * centre - near_weight * near + corner_weight * corner + distant_weight * distant
    return centre + damping * (data_moment - applied - data_weight * centre) / (centre_weight + data_weight)


def reference(start, dest_tile, cell_row, cell_col, source_type, sounding_value, sounding_weight, type_gain):
    factor = type_gain[source_type]
    scaled = sounding_weight * factor
    moment = scaled * sounding_value
    grid_rows = (dest_tile // N_COL) * TR + cell_row
    grid_cols = (dest_tile % N_COL) * TC + cell_col
    grid_weight = jnp.zeros((NR, NC), jnp.float32).at[grid_rows, grid_cols].add(scaled)
    grid_moment = jnp.zeros((NR, NC), jnp.float32).at[grid_rows, grid_cols].add(moment)
    current = start
    for level in range(SWEEPS):
        current = relax_step(jnp.pad(current, 2), grid_weight, grid_moment)
    return current
```

```python
import functools

import jax
import jax.numpy as jnp
from jax import lax
from jax.experimental import pallas as pl
from jax.experimental.pallas import tpu as pltpu
from jax.sharding import PartitionSpec as P

SWEEPS = 4
LANES = 128
HALO = 2 * SWEEPS
MARGIN = 8
MESH = pl.DeviceIdType.MESH

tension = 0.35
centre_weight = 20.0 * (1.0 - tension) + 4.0 * tension
near_weight = 8.0 * (1.0 - tension) + tension
corner_weight = 2.0 * (1.0 - tension)
distant_weight = 1.0 - tension
damping = 0.5

f32 = jnp.float32
bf16 = jnp.bfloat16
NT = (((1,), (1,)), ((), ()))


def two_pieces(x):
    high = x.astype(bf16).astype(f32)
    return high, x - high


def kernel(
    row_count, blocks, start, dest, cell_row, cell_col, source, value, weight, gain, out,
    outbox, inbox, left_route, right_route, routed, slots, pieces, left, right, total,
    field, grid, send_sem, recv_sem, halo_send, halo_recv, grid_send, grid_recv,
):
    tile_rows, tile_cols = start.shape
    sounding_rows = dest.shape[0]
    tiles = 2 * row_count
    my_row, my_col = lax.axis_index("row"), lax.axis_index("col")
    me = 2 * my_row + my_col
    other = 1 - my_col
    ext_rows = tile_rows + 2 * HALO
    interior = pl.ds(MARGIN + HALO, tile_rows)

    barrier = pltpu.get_barrier_semaphore()

    def greet(step, carry):
        peer = lax.rem(me + step, tiles)
        pl.semaphore_signal(
            barrier, inc=1, device_id={"row": peer // 2, "col": lax.rem(peer, 2)},
            device_id_type=MESH,
        )
        return carry

    lax.fori_loop(1, tiles, greet, 0)

    destination = dest[...]
    lane_a = lax.broadcasted_iota(jnp.int32, (LANES, 2 * LANES), 0)
    lane_b = lax.broadcasted_iota(jnp.int32, (LANES, 2 * LANES), 1)
    before = jnp.where((lane_a < lane_b) | (lane_b >= LANES), 1.0, 0.0).astype(bf16)
    sub_a = lax.broadcasted_iota(jnp.int32, (sounding_rows, sounding_rows), 0)
    sub_b = lax.broadcasted_iota(jnp.int32, (sounding_rows, sounding_rows), 1)
    above = jnp.where(sub_b < sub_a, 1.0, 0.0).astype(bf16)

    def rank_of(tile, rank):
        hit = jnp.where(destination == tile, 1.0, 0.0)
        both = jnp.dot(hit.astype(bf16), before, preferred_element_type=f32)
        earlier = jnp.dot(
            above, both[:, LANES:].astype(bf16), preferred_element_type=f32
        )
        return rank + hit * (both[:, :LANES] + earlier)

    rank = jnp.zeros(destination.shape, f32)
    if tiles <= 16:
        for tile in range(tiles):
            rank = rank_of(tile, rank)
    else:
        rank = lax.fori_loop(0, tiles, rank_of, rank)
    rank = rank.astype(jnp.int32)
    slots[0] = (destination >> 1) * blocks + (rank >> 7)
    slots[1] = (destination & 1) * LANES + (rank & (LANES - 1))
    kind = source[...]
    factor = jnp.where(kind == 0, gain[0], jnp.where(kind == 1, gain[1], gain[2]))
    scaled = weight[...] * factor
    moment = scaled * value[...]
    pieces[0], pieces[1] = two_pieces(scaled)
    pieces[2], pieces[3] = two_pieces(moment)
    column = cell_col[...]
    pieces[4] = (cell_row[...] * 4 + (column >> 9)).astype(f32)
    pieces[5] = ((column & 511) - 256).astype(f32)

    slot_rows = row_count * blocks
    slot_ids = lax.broadcasted_iota(jnp.int32, (slot_rows, LANES), 0)
    lane_ids = lax.broadcasted_iota(jnp.int32, (2 * LANES, LANES), 0)
    routed[...] = jnp.zeros(routed.shape, f32)

    def place(step, carry):
        for r in range(8):
            here = pl.ds(step * 8 + r, 1)
            lanes = slice(r * LANES, (r + 1) * LANES)
            chosen = slot_ids == slots[0, here, :]
            left_route[:, lanes] = jnp.concatenate(
                [jnp.where(chosen, pieces[p, here, :], 0.0) for p in range(6)], axis=0
            ).astype(bf16)
            right_route[:, lanes] = jnp.where(
                lane_ids == slots[1, here, :], 1.0, 0.0
            ).astype(bf16)
        routed[...] += lax.dot_general(
            left_route[...], right_route[...], NT, preferred_element_type=f32
        )
        return carry

    lax.fori_loop(0, sounding_rows // 8, place, 0)

    def piece(p):
        return routed[p * slot_rows : (p + 1) * slot_rows, :]

    packed = piece(4)
    placed_row = jnp.floor(packed * 0.25)
    placed_col = (packed - 4.0 * placed_row) * 512.0 + (piece(5) + 256.0)
    values = (piece(0) + piece(1), piece(2) + piece(3), placed_row, placed_col)
    for v in range(4):
        for r in range(row_count):
            for c in range(2):
                outbox[2 * r + c, v * blocks : (v + 1) * blocks, :] = values[v][
                    r * blocks : (r + 1) * blocks, c * LANES : (c + 1) * LANES
                ]

    pl.semaphore_wait(barrier, tiles - 1)

    def sounding_copy(peer):
        return pltpu.make_async_remote_copy(
            src_ref=outbox.at[peer], dst_ref=inbox.at[me],
            send_sem=send_sem.at[peer], recv_sem=recv_sem.at[me],
            device_id={"row": peer // 2, "col": lax.rem(peer, 2)}, device_id_type=MESH,
        )

    def arrived(origin):
        pltpu.make_async_remote_copy(
            src_ref=outbox.at[origin], dst_ref=inbox.at[origin],
            send_sem=send_sem.at[origin], recv_sem=recv_sem.at[origin],
            device_id={"row": origin // 2, "col": lax.rem(origin, 2)}, device_id_type=MESH,
        ).wait_recv()

    sounding_copy(2 * my_row + other).start()

    def send(step, carry):
        peer_row = lax.rem(my_row + row_count - step, row_count)
        sounding_copy(2 * peer_row + my_col).start()
        sounding_copy(2 * peer_row + other).start()
        return carry

    lax.fori_loop(1, row_count, send, 0)

    strip = pl.ds(pl.multiple_of((1 - my_col) * (tile_cols - LANES), LANES), LANES)
    side = pl.ds(tile_cols, LANES)
    body = pl.ds(0, tile_cols)
    top, bottom = pl.ds(MARGIN, HALO), pl.ds(MARGIN + HALO + tile_rows, HALO)
    has_up, has_down = my_row > 0, my_row < row_count - 1

    def halo_copies(cut, put, sends, recvs):
        first, last = (0, HALO), (tile_rows - HALO, HALO)
        plan = (
            (has_up, -1, my_col, first, body, bottom, body),
            (has_down, 1, my_col, last, body, top, body),
            (None, 0, other, (0, tile_rows), strip, interior, side),
            (has_up, -1, other, first, strip, bottom, side),
            (has_down, 1, other, last, strip, top, side),
        )
        return [
            (
                condition,
                pltpu.make_async_remote_copy(
                    src_ref=cut(rows, columns), dst_ref=put(to_rows, to_columns),
                    send_sem=sends.at[n], recv_sem=recvs.at[n],
                    device_id={
                        "row": jnp.clip(my_row + shift, 0, row_count - 1),
                        "col": to_col,
                    },
                    device_id_type=MESH,
                ),
            )
            for n, (condition, shift, to_col, rows, columns, to_rows, to_columns) in enumerate(plan)
        ]

    def under(condition, action):
        if condition is None:
            action()
        else:
            pl.when(condition)(action)

    mirrored = (has_down, has_up, None, has_down, has_up)

    def finish(copies):
        for (condition, copy), from_there in zip(copies, mirrored):
            under(condition, copy.wait_send)
            under(from_there, copy.wait_recv)

    field_copies = halo_copies(
        lambda rows, columns: start.at[pl.ds(*rows), columns],
        lambda rows, columns: field.at[0, rows, columns],
        halo_send, halo_recv,
    )
    for condition, copy in field_copies:
        under(condition, copy.start)

    def blank(rows):
        def action():
            field[0, rows, :] = jnp.zeros((HALO, field.shape[2]), f32)
            grid[:, rows, :] = jnp.zeros((2, HALO, field.shape[2]), f32)
        return action

    pl.when(jnp.logical_not(has_up))(blank(top))
    pl.when(jnp.logical_not(has_down))(blank(bottom))
    for n in range(2):
        field[n, :MARGIN, :] = jnp.zeros((MARGIN, field.shape[2]), f32)
        field[n, MARGIN + ext_rows :, :] = jnp.zeros((MARGIN, field.shape[2]), f32)
    field[0, interior, :tile_cols] = start[...]

    row_ids = lax.broadcasted_iota(jnp.int32, (tile_rows, LANES), 0).astype(f32)
    col_ids = lax.broadcasted_iota(jnp.int32, (LANES, LANES), 0).astype(f32)
    chunks = tile_cols // LANES

    def grid_pair(source_row, first):
        for c in range(2):
            origin = 2 * source_row + c
            for b in range(blocks):
                lanes = slice((c * blocks + b) * LANES, (c * blocks + b + 1) * LANES)
                w, m, r, k = (
                    inbox[origin, v * blocks + b : v * blocks + b + 1, :] for v in range(4)
                )
                (w_high, w_low), (m_high, m_low) = two_pieces(w), two_pieces(m)
                chosen = row_ids == r
                left[:, lanes] = jnp.concatenate(
                    [jnp.where(chosen, x, 0.0) for x in (w_high, m_high, w_low, m_low)], axis=0
                ).astype(bf16)
                chunk = jnp.floor(k * (1.0 / LANES))
                base = jnp.where(col_ids == k - LANES * chunk, 1.0, 0.0).astype(bf16)
                base = base.reshape(LANES // 16, 16, LANES)
                chunk = jnp.broadcast_to(chunk, (16, LANES))
                for n in range(chunks):
                    mask = jnp.where(chunk == float(n), 1.0, 0.0).astype(bf16)
                    right[n * LANES : (n + 1) * LANES, lanes] = (base * mask[None]).reshape(
                        LANES, LANES
                    )
        term = lax.dot_general(right[...], left[...], NT, preferred_element_type=f32)
        if first:
            total[...] = term
        else:
            total[...] += term

    inbox[me] = outbox[me]
    arrived(2 * my_row + other)
    grid_pair(my_row, True)

    def grid_step(step, carry):
        source_row = lax.rem(my_row + step, row_count)
        arrived(2 * source_row)
        arrived(2 * source_row + 1)
        grid_pair(source_row, False)
        return carry

    lax.fori_loop(1, row_count, grid_step, 0)

    half = 2 * tile_rows
    for n in range(chunks):
        part = total[n * LANES : (n + 1) * LANES, :]
        both = (part[:, :half] + part[:, half:]).T
        lanes = slice(n * LANES, (n + 1) * LANES)
        scale = damping / (centre_weight + both[:tile_rows])
        grid[0, interior, lanes] = scale
        grid[1, interior, lanes] = scale * both[tile_rows:]

    grid_copies = halo_copies(
        lambda rows, columns: grid.at[:, pl.ds(MARGIN + HALO + rows[0], rows[1]), columns],
        lambda rows, columns: grid.at[:, rows, columns],
        grid_send, grid_recv,
    )
    for condition, copy in grid_copies:
        under(condition, copy.start)

    def sent(step, carry):
        peer = lax.rem(me + step, tiles)
        sounding_copy(peer).wait_send()
        return carry

    lax.fori_loop(1, tiles, sent, 0)
    finish(field_copies)
    finish(grid_copies)

    strip_lane = lax.broadcasted_iota(jnp.int32, (ext_rows, LANES), 1)
    nearer = (strip_lane < LANES // 2) == (my_col == 0)
    ext = slice(MARGIN, MARGIN + ext_rows)
    field[0, ext, tile_cols:] = jnp.where(nearer, field[0, ext, tile_cols:], 0.0)
    for n in range(2):
        grid[n, ext, tile_cols:] = jnp.where(nearer, grid[n, ext, tile_cols:], 0.0)

    width = field.shape[2]

    def relaxed(now, at):
        centre = field[now, at : at + 8, :]
        ring = field[now, at - 1 : at + 7, :] + field[now, at + 1 : at + 9, :]
        far = field[now, at - 2 : at + 6, :] + field[now, at + 2 : at + 10, :]
        beside = near_weight * centre - corner_weight * ring
        beside = pltpu.roll(beside, 1, 1) + pltpu.roll(beside, width - 1, 1)
        far = far + (pltpu.roll(centre, 2, 1) + pltpu.roll(centre, width - 2, 1))
        pull = near_weight * ring + beside - distant_weight * far
        return 0.5 * centre + (grid[1, at : at + 8, :] + grid[0, at : at + 8, :] * pull)

    def sweep(level, carry):
        now = lax.rem(level, 2)
        for at in range(MARGIN, MARGIN + ext_rows, 8):
            field[1 - now, at : at + 8, :] = relaxed(now, at)
        return carry

    lax.fori_loop(0, SWEEPS - 1, sweep, 0)
    for at in range(MARGIN + HALO, MARGIN + HALO + tile_rows, 8):
        new = relaxed((SWEEPS - 1) % 2, at)
        out[at - MARGIN - HALO : at - MARGIN - HALO + 8, :] = new[:, :tile_cols]


def body(
    start, dest_tile, cell_row, cell_col, source_type, sounding_value, sounding_weight, type_gain
):
    tile_rows, tile_cols = start.shape
    row_count = lax.axis_size("row")
    assert lax.axis_size("col") == 2
    assert tile_rows == 64 and tile_cols <= 2048 and tile_cols % LANES == 0
    count = dest_tile.shape[0]
    assert count % (8 * LANES) == 0
    sounding_rows = count // LANES
    tiles = 2 * row_count
    capacity = 5 * count // (4 * tiles)
    blocks = -(-capacity // LANES)
    box_rows = -(-4 * blocks // 8) * 8
    slot_rows = row_count * blocks
    width = tile_cols + LANES
    tall = tile_rows + 2 * HALO + 2 * MARGIN
    depth = 2 * blocks * LANES
    vmem = pl.BlockSpec(memory_space=pltpu.VMEM)
    call = pl.pallas_call(
        functools.partial(kernel, row_count, blocks),
        out_shape=jax.ShapeDtypeStruct(start.shape, f32),
        in_specs=[vmem] * 7 + [pl.BlockSpec(memory_space=pltpu.SMEM)],
        out_specs=vmem,
        scratch_shapes=[
            pltpu.VMEM((tiles, box_rows, LANES), f32),
            pltpu.VMEM((tiles, box_rows, LANES), f32),
            pltpu.VMEM((6 * slot_rows, 8 * LANES), bf16),
            pltpu.VMEM((2 * LANES, 8 * LANES), bf16),
            pltpu.VMEM((6 * slot_rows, 2 * LANES), f32),
            pltpu.VMEM((2, sounding_rows, LANES), jnp.int32),
            pltpu.VMEM((6, sounding_rows, LANES), f32),
            pltpu.VMEM((4 * tile_rows, depth), bf16),
            pltpu.VMEM((tile_cols, depth), bf16),
            pltpu.VMEM((tile_cols, 4 * tile_rows), f32),
            pltpu.VMEM((2, tall, width), f32),
            pltpu.VMEM((2, tall, width), f32),
            pltpu.SemaphoreType.DMA((tiles,)),
            pltpu.SemaphoreType.DMA((tiles,)),
            pltpu.SemaphoreType.DMA((5,)),
            pltpu.SemaphoreType.DMA((5,)),
            pltpu.SemaphoreType.DMA((5,)),
            pltpu.SemaphoreType.DMA((5,)),
        ],
        compiler_params=pltpu.CompilerParams(
            collective_id=0, has_side_effects=True, vmem_limit_bytes=48 * 1024 * 1024
        ),
    )
    shaped = (sounding_rows, LANES)
    return call(
        start, dest_tile.reshape(shaped), cell_row.reshape(shaped), cell_col.reshape(shaped),
        source_type.reshape(shaped), sounding_value.reshape(shaped),
        sounding_weight.reshape(shaped), type_gain,
    )


def solution(mesh):
    many = P(("slab", "row", "col"))
    in_specs = (P(("slab", "row"), "col"), many, many, many, many, many, many, P())
    out_specs = P(("slab", "row"), "col")
    return jax.shard_map(body, mesh=mesh, in_specs=in_specs, out_specs=out_specs, check_vma=False)
```

```python
import functools

import jax
import jax.numpy as jnp
from jax import lax
from jax.experimental import pallas as pl
from jax.experimental.pallas import tpu as pltpu
from jax.sharding import PartitionSpec as P

SWEEPS = 4
LANES = 128
HALO = 2 * SWEEPS
MARGIN = 8
MESH = pl.DeviceIdType.MESH

tension = 0.35
centre_weight = 20.0 * (1.0 - tension) + 4.0 * tension
near_weight = 8.0 * (1.0 - tension) + tension
corner_weight = 2.0 * (1.0 - tension)
distant_weight = 1.0 - tension
damping = 0.5

f32 = jnp.float32
bf16 = jnp.bfloat16
NT = (((1,), (1,)), ((), ()))


def two_pieces(x):
    high = x.astype(bf16).astype(f32)
    return high, x - high


def kernel(row_count, blocks, start, *refs):
    soundings, gain_in, out = refs[:6], refs[6], refs[7]
    whole_numbers, reals, gain, load_sem = refs[8:12]
    dest, cell_row, cell_col, source = (whole_numbers.at[n] for n in range(4))
    value, weight = (reals.at[n] for n in range(2))
    (
        outbox, inbox, left_route, right_route, routed, slots, pieces,
        left, right, total, field, grid, send_sem,
        recv_sem, halo_send, halo_recv, grid_send, grid_recv,
    ) = refs[12:]
    tile_rows, tile_cols = start.shape
    sounding_rows = dest.shape[0]
    tiles = 2 * row_count
    my_row, my_col = lax.axis_index("row"), lax.axis_index("col")
    me = 2 * my_row + my_col
    other = 1 - my_col
    ext_rows = tile_rows + 2 * HALO
    interior = pl.ds(MARGIN + HALO, tile_rows)

    loads = [
        pltpu.make_async_copy(array, place, load_sem.at[n])
        for n, (array, place) in enumerate(
            zip(soundings, (dest, cell_row, cell_col, source, value, weight))
        )
    ]
    loads.append(pltpu.make_async_copy(gain_in, gain, load_sem.at[6]))
    start_load = pltpu.make_async_copy(
        start, field.at[0, interior, pl.ds(0, tile_cols)], load_sem.at[7]
    )
    for load in loads:
        load.start()
    start_load.start()

    barrier = pltpu.get_barrier_semaphore()

    def greet(step, carry):
        peer = lax.rem(me + step, tiles)
        pl.semaphore_signal(
            barrier, inc=1, device_id={"row": peer // 2, "col": lax.rem(peer, 2)},
            device_id_type=MESH,
        )
        return carry

    lax.fori_loop(1, tiles, greet, 0)

    for load in loads:
        load.wait()
    destination = dest[...]
    lane_a = lax.broadcasted_iota(jnp.int32, (LANES, 2 * LANES), 0)
    lane_b = lax.broadcasted_iota(jnp.int32, (LANES, 2 * LANES), 1)
    before = jnp.where((lane_a < lane_b) | (lane_b >= LANES), 1.0, 0.0).astype(bf16)
    sub_a = lax.broadcasted_iota(jnp.int32, (sounding_rows, sounding_rows), 0)
    sub_b = lax.broadcasted_iota(jnp.int32, (sounding_rows, sounding_rows), 1)
    above = jnp.where(sub_b < sub_a, 1.0, 0.0).astype(bf16)

    def rank_of(tile, rank):
        hit = jnp.where(destination == tile, 1.0, 0.0)
        both = jnp.dot(hit.astype(bf16), before, preferred_element_type=f32)
        earlier = jnp.dot(
            above, both[:, LANES:].astype(bf16), preferred_element_type=f32
        )
        return rank + hit * (both[:, :LANES] + earlier)

    rank = jnp.zeros(destination.shape, f32)
    if tiles <= 16:
        for tile in range(tiles):
            rank = rank_of(tile, rank)
    else:
        rank = lax.fori_loop(0, tiles, rank_of, rank)
    rank = rank.astype(jnp.int32)
    slots[0] = (destination >> 1) * blocks + (rank >> 7)
    slots[1] = (destination & 1) * LANES + (rank & (LANES - 1))
    kind = source[...]
    factor = jnp.where(kind == 0, gain[0], jnp.where(kind == 1, gain[1], gain[2]))
    scaled = weight[...] * factor
    moment = scaled * value[...]
    pieces[0], pieces[1] = two_pieces(scaled)
    pieces[2], pieces[3] = two_pieces(moment)
    column = cell_col[...]
    pieces[4] = (cell_row[...] * 4 + (column >> 9)).astype(f32)
    pieces[5] = ((column & 511) - 256).astype(f32)

    slot_rows = row_count * blocks
    slot_ids = lax.broadcasted_iota(jnp.int32, (slot_rows, LANES), 0)
    lane_ids = lax.broadcasted_iota(jnp.int32, (2 * LANES, LANES), 0)
    routed[...] = jnp.zeros(routed.shape, f32)

    def place(step, carry):
        for r in range(8):
            here = pl.ds(step * 8 + r, 1)
            lanes = slice(r * LANES, (r + 1) * LANES)
            chosen = slot_ids == slots[0, here, :]
            left_route[:, lanes] = jnp.concatenate(
                [jnp.where(chosen, pieces[p, here, :], 0.0) for p in range(6)], axis=0
            ).astype(bf16)
            right_route[:, lanes] = jnp.where(
                lane_ids == slots[1, here, :], 1.0, 0.0
            ).astype(bf16)
        routed[...] += lax.dot_general(
            left_route[...], right_route[...], NT, preferred_element_type=f32
        )
        return carry

    lax.fori_loop(0, sounding_rows // 8, place, 0)

    def piece(p):
        return routed[p * slot_rows : (p + 1) * slot_rows, :]

    packed = piece(4)
    placed_row = jnp.floor(packed * 0.25)
    placed_col = (packed - 4.0 * placed_row) * 512.0 + (piece(5) + 256.0)
    values = (piece(0) + piece(1), piece(2) + piece(3), placed_row, placed_col)
    for v in range(4):
        for r in range(row_count):
            for c in range(2):
                outbox[2 * r + c, v * blocks : (v + 1) * blocks, :] = values[v][
                    r * blocks : (r + 1) * blocks, c * LANES : (c + 1) * LANES
                ]

    pl.semaphore_wait(barrier, tiles - 1)

    def sounding_copy(peer):
        return pltpu.make_async_remote_copy(
            src_ref=outbox.at[peer], dst_ref=inbox.at[me],
            send_sem=send_sem.at[peer], recv_sem=recv_sem.at[me],
            device_id={"row": peer // 2, "col": lax.rem(peer, 2)}, device_id_type=MESH,
        )

    def arrived(origin):
        pltpu.make_async_remote_copy(
            src_ref=outbox.at[origin], dst_ref=inbox.at[origin],
            send_sem=send_sem.at[origin], recv_sem=recv_sem.at[origin],
            device_id={"row": origin // 2, "col": lax.rem(origin, 2)}, device_id_type=MESH,
        ).wait_recv()

    sounding_copy(2 * my_row + other).start()

    def send(step, carry):
        peer_row = lax.rem(my_row + row_count - step, row_count)
        sounding_copy(2 * peer_row + my_col).start()
        sounding_copy(2 * peer_row + other).start()
        return carry

    lax.fori_loop(1, row_count, send, 0)

    strip = pl.ds(pl.multiple_of((1 - my_col) * (tile_cols - LANES), LANES), LANES)
    side = pl.ds(tile_cols, LANES)
    body = pl.ds(0, tile_cols)
    top, bottom = pl.ds(MARGIN, HALO), pl.ds(MARGIN + HALO + tile_rows, HALO)
    has_up, has_down = my_row > 0, my_row < row_count - 1

    def halo_copies(cut, put, sends, recvs):
        first, last = (0, HALO), (tile_rows - HALO, HALO)
        plan = (
            (has_up, -1, my_col, first, body, bottom, body),
            (has_down, 1, my_col, last, body, top, body),
            (None, 0, other, (0, tile_rows), strip, interior, side),
            (has_up, -1, other, first, strip, bottom, side),
            (has_down, 1, other, last, strip, top, side),
        )
        return [
            (
                condition,
                pltpu.make_async_remote_copy(
                    src_ref=cut(rows, columns), dst_ref=put(to_rows, to_columns),
                    send_sem=sends.at[n], recv_sem=recvs.at[n],
                    device_id={
                        "row": jnp.clip(my_row + shift, 0, row_count - 1),
                        "col": to_col,
                    },
                    device_id_type=MESH,
                ),
            )
            for n, (condition, shift, to_col, rows, columns, to_rows, to_columns) in enumerate(plan)
        ]

    def under(condition, action):
        if condition is None:
            action()
        else:
            pl.when(condition)(action)

    mirrored = (has_down, has_up, None, has_down, has_up)

    def finish(copies, which=range(5)):
        for (condition, copy), n in zip(copies, which):
            from_there = mirrored[n]
            under(condition, copy.wait_send)
            under(from_there, copy.wait_recv)

    field_copies = halo_copies(
        lambda rows, columns: start.at[pl.ds(*rows), columns],
        lambda rows, columns: field.at[0, rows, columns],
        halo_send, halo_recv,
    )
    for condition, copy in field_copies:
        under(condition, copy.start)

    def blank(rows):
        def action():
            field[0, rows, :] = jnp.zeros((HALO, field.shape[2]), f32)
            grid[:, rows, :] = jnp.zeros((2, HALO, field.shape[2]), f32)
        return action

    pl.when(jnp.logical_not(has_up))(blank(top))
    pl.when(jnp.logical_not(has_down))(blank(bottom))
    for n in range(SWEEPS):
        field[n, :MARGIN, :] = jnp.zeros((MARGIN, field.shape[2]), f32)
        field[n, MARGIN + ext_rows :, :] = jnp.zeros((MARGIN, field.shape[2]), f32)
    start_load.wait()

    row_ids = lax.broadcasted_iota(jnp.int32, (tile_rows, LANES), 0).astype(f32)
    col_ids = lax.broadcasted_iota(jnp.int32, (LANES, LANES), 0).astype(f32)
    chunks = tile_cols // LANES

    def grid_pair(source_row, first):
        for c in range(2):
            origin = 2 * source_row + c
            for b in range(blocks):
                lanes = slice((c * blocks + b) * LANES, (c * blocks + b + 1) * LANES)
                w, m, r, k = (
                    inbox[origin, v * blocks + b : v * blocks + b + 1, :] for v in range(4)
                )
                (w_high, w_low), (m_high, m_low) = two_pieces(w), two_pieces(m)
                chosen = row_ids == r
                left[:, lanes] = jnp.concatenate(
                    [jnp.where(chosen, x, 0.0) for x in (w_high, m_high, w_low, m_low)], axis=0
                ).astype(bf16)
                chunk = jnp.floor(k * (1.0 / LANES))
                base = jnp.where(col_ids == k - LANES * chunk, 1.0, 0.0).astype(bf16)
                base = base.reshape(LANES // 16, 16, LANES)
                chunk = jnp.broadcast_to(chunk, (16, LANES))
                for n in range(chunks):
                    mask = jnp.where(chunk == float(n), 1.0, 0.0).astype(bf16)
                    right[n * LANES : (n + 1) * LANES, lanes] = (base * mask[None]).reshape(
                        LANES, LANES
                    )
        term = lax.dot_general(right[...], left[...], NT, preferred_element_type=f32)
        if first:
            total[...] = term
        else:
            total[...] += term

    inbox[me] = outbox[me]
    arrived(2 * my_row + other)
    grid_pair(my_row, True)

    def grid_step(step, carry):
        source_row = lax.rem(my_row + step, row_count)
        arrived(2 * source_row)
        arrived(2 * source_row + 1)
        grid_pair(source_row, False)
        return carry

    lax.fori_loop(1, row_count, grid_step, 0)

    half = 2 * tile_rows
    for n in range(chunks):
        part = total[n * LANES : (n + 1) * LANES, :]
        both = (part[:, :half] + part[:, half:]).T
        lanes = slice(n * LANES, (n + 1) * LANES)
        scale = damping / (centre_weight + both[:tile_rows])
        grid[0, interior, lanes] = scale
        grid[1, interior, lanes] = scale * both[tile_rows:]

    grid_copies = halo_copies(
        lambda rows, columns: grid.at[:, pl.ds(MARGIN + HALO + rows[0], rows[1]), columns],
        lambda rows, columns: grid.at[:, rows, columns],
        grid_send, grid_recv,
    )
    for n in (2, 0, 1, 3, 4):
        under(grid_copies[n][0], grid_copies[n][1].start)

    def sent(step, carry):
        peer = lax.rem(me + step, tiles)
        sounding_copy(peer).wait_send()
        return carry

    lax.fori_loop(1, tiles, sent, 0)
    finish(field_copies)
    grid_copies[2][1].wait()

    def keep_nearer(ref, rows, n):
        strip_lane = lax.broadcasted_iota(jnp.int32, (rows.stop - rows.start, LANES), 1)
        nearer = (strip_lane < LANES // 2) == (my_col == 0)
        ref[n, rows, tile_cols:] = jnp.where(nearer, ref[n, rows, tile_cols:], 0.0)

    first_row, last_row = MARGIN + HALO, MARGIN + HALO + tile_rows
    keep_nearer(field, slice(MARGIN, MARGIN + ext_rows), 0)
    for n in range(2):
        keep_nearer(grid, slice(first_row, last_row), n)

    width = field.shape[2]

    def relaxed(now, at):
        centre = field[now, at : at + 8, :]
        ring = field[now, at - 1 : at + 7, :] + field[now, at + 1 : at + 9, :]
        far = field[now, at - 2 : at + 6, :] + field[now, at + 2 : at + 10, :]
        beside = near_weight * centre - corner_weight * ring
        beside = pltpu.roll(beside, 1, 1) + pltpu.roll(beside, width - 1, 1)
        far = far + (pltpu.roll(centre, 2, 1) + pltpu.roll(centre, width - 2, 1))
        pull = near_weight * ring + beside - distant_weight * far
        return 0.5 * centre + (grid[1, at : at + 8, :] + grid[0, at : at + 8, :] * pull)

    def update(level, rows):
        for at in rows:
            field[level + 1, at : at + 8, :] = relaxed(level, at)

    def finished(rows):
        for at in rows:
            new = relaxed(SWEEPS - 1, at)
            out[at - first_row : at - first_row + 8, :] = new[:, :tile_cols]

    def inner(level, carry):
        update(level, range(first_row, last_row, 8))
        return carry

    lax.fori_loop(0, SWEEPS - 1, inner, 0)
    finished(range(first_row + 8, last_row - 8, 8))

    finish([(c, k) for n, (c, k) in enumerate(grid_copies) if n != 2], (0, 1, 3, 4))
    for rows in (slice(MARGIN, first_row), slice(last_row, last_row + HALO)):
        for n in range(2):
            keep_nearer(grid, rows, n)
    edges = (first_row - 8, last_row)
    ends = (first_row, last_row - 8)
    update(0, edges)

    def outer(level, carry):
        update(level, edges + ends)
        return carry

    lax.fori_loop(1, SWEEPS - 1, outer, 0)
    finished(ends)


def body(
    start, dest_tile, cell_row, cell_col, source_type, sounding_value, sounding_weight, type_gain
):
    tile_rows, tile_cols = start.shape
    row_count = lax.axis_size("row")
    assert lax.axis_size("col") == 2
    assert tile_rows == 64 and tile_cols <= 2048 and tile_cols % LANES == 0
    count = dest_tile.shape[0]
    assert count % (8 * LANES) == 0
    sounding_rows = count // LANES
    tiles = 2 * row_count
    capacity = 5 * count // (4 * tiles)
    blocks = -(-capacity // LANES)
    box_rows = -(-4 * blocks // 8) * 8
    slot_rows = row_count * blocks
    width = tile_cols + LANES
    tall = tile_rows + 2 * HALO + 2 * MARGIN
    depth = 2 * blocks * LANES
    vmem = pl.BlockSpec(memory_space=pltpu.VMEM)
    call = pl.pallas_call(
        functools.partial(kernel, row_count, blocks),
        out_shape=jax.ShapeDtypeStruct(start.shape, f32),
        in_specs=[pl.BlockSpec(memory_space=pltpu.HBM)] * 8,
        out_specs=vmem,
        scratch_shapes=[
            pltpu.VMEM((4, sounding_rows, LANES), jnp.int32),
            pltpu.VMEM((2, sounding_rows, LANES), f32),
            pltpu.SMEM((3,), f32),
            pltpu.SemaphoreType.DMA((8,)),
            pltpu.VMEM((tiles, box_rows, LANES), f32),
            pltpu.VMEM((tiles, box_rows, LANES), f32),
            pltpu.VMEM((6 * slot_rows, 8 * LANES), bf16),
            pltpu.VMEM((2 * LANES, 8 * LANES), bf16),
            pltpu.VMEM((6 * slot_rows, 2 * LANES), f32),
            pltpu.VMEM((2, sounding_rows, LANES), jnp.int32),
            pltpu.VMEM((6, sounding_rows, LANES), f32),
            pltpu.VMEM((4 * tile_rows, depth), bf16),
            pltpu.VMEM((tile_cols, depth), bf16),
            pltpu.VMEM((tile_cols, 4 * tile_rows), f32),
            pltpu.VMEM((SWEEPS, tall, width), f32),
            pltpu.VMEM((2, tall, width), f32),
            pltpu.SemaphoreType.DMA((tiles,)),
            pltpu.SemaphoreType.DMA((tiles,)),
            pltpu.SemaphoreType.DMA((5,)),
            pltpu.SemaphoreType.DMA((5,)),
            pltpu.SemaphoreType.DMA((5,)),
            pltpu.SemaphoreType.DMA((5,)),
        ],
        compiler_params=pltpu.CompilerParams(
            collective_id=0, has_side_effects=True, vmem_limit_bytes=48 * 1024 * 1024
        ),
    )
    shaped = (sounding_rows, LANES)
    return call(
        start, dest_tile.reshape(shaped), cell_row.reshape(shaped), cell_col.reshape(shaped),
        source_type.reshape(shaped), sounding_value.reshape(shaped),
        sounding_weight.reshape(shaped), type_gain,
    )


def solution(mesh):
    many = P(("slab", "row", "col"))
    in_specs = (P(("slab", "row"), "col"), many, many, many, many, many, many, P())
    out_specs = P(("slab", "row"), "col")
    return jax.shard_map(body, mesh=mesh, in_specs=in_specs, out_specs=out_specs, check_vma=False)
```

```python
import functools

import jax
import jax.numpy as jnp
from jax import lax
from jax.experimental import pallas as pl
from jax.experimental.pallas import tpu as pltpu
from jax.sharding import PartitionSpec as P

SWEEPS = 4
PARTS = 4
LATE = 4
LANES = 128
HALO = 2 * SWEEPS
MARGIN = 8
MESH = pl.DeviceIdType.MESH

tension = 0.35
centre_weight = 20.0 * (1.0 - tension) + 4.0 * tension
near_weight = 8.0 * (1.0 - tension) + tension
corner_weight = 2.0 * (1.0 - tension)
distant_weight = 1.0 - tension
damping = 0.5

f32 = jnp.float32
bf16 = jnp.bfloat16
NT = (((1,), (1,)), ((), ()))


def two_pieces(x):
    high = x.astype(bf16).astype(f32)
    return high, x - high


def kernel(row_count, blocks, start, *refs):
    soundings, gain_in, out = refs[:6], refs[6], refs[7]
    whole_numbers, reals, gain, load_sem = refs[8:12]
    dest, cell_row, cell_col, source = (whole_numbers.at[n] for n in range(4))
    value, weight = (reals.at[n] for n in range(2))
    (
        outbox, inbox, left_route, right_route, routed, slots, pieces,
        left, base, chunk_of, right, right_late, total, field, grid, send_sem,
        recv_sem, halo_send, halo_recv, grid_send, grid_recv, row_send, row_recv,
    ) = refs[12:]
    tile_rows, tile_cols = start.shape
    sounding_rows = dest.shape[0]
    tiles = 2 * row_count
    my_row, my_col = lax.axis_index("row"), lax.axis_index("col")
    me = 2 * my_row + my_col
    other = 1 - my_col
    ext_rows = tile_rows + 2 * HALO
    interior = pl.ds(MARGIN + HALO, tile_rows)

    loads = [
        pltpu.make_async_copy(array, place, load_sem.at[n])
        for n, (array, place) in enumerate(
            zip(soundings, (dest, cell_row, cell_col, source, value, weight))
        )
    ]
    loads.append(pltpu.make_async_copy(gain_in, gain, load_sem.at[6]))
    start_load = pltpu.make_async_copy(
        start, field.at[0, interior, pl.ds(0, tile_cols)], load_sem.at[7]
    )
    for load in loads:
        load.start()
    start_load.start()

    barrier = pltpu.get_barrier_semaphore()

    def greet(step, carry):
        peer = lax.rem(me + step, tiles)
        pl.semaphore_signal(
            barrier, inc=1, device_id={"row": peer // 2, "col": lax.rem(peer, 2)},
            device_id_type=MESH,
        )
        return carry

    lax.fori_loop(1, tiles, greet, 0)

    for load in loads:
        load.wait()
    destination = dest[...]
    lane_a = lax.broadcasted_iota(jnp.int32, (LANES, 2 * LANES), 0)
    lane_b = lax.broadcasted_iota(jnp.int32, (LANES, 2 * LANES), 1)
    before = jnp.where((lane_a < lane_b) | (lane_b >= LANES), 1.0, 0.0).astype(bf16)
    sub_a = lax.broadcasted_iota(jnp.int32, (sounding_rows, sounding_rows), 0)
    sub_b = lax.broadcasted_iota(jnp.int32, (sounding_rows, sounding_rows), 1)
    above = jnp.where(sub_b < sub_a, 1.0, 0.0).astype(bf16)

    def rank_of(tile, rank):
        hit = jnp.where(destination == tile, 1.0, 0.0)
        both = jnp.dot(hit.astype(bf16), before, preferred_element_type=f32)
        earlier = jnp.dot(
            above, both[:, LANES:].astype(bf16), preferred_element_type=f32
        )
        return rank + hit * (both[:, :LANES] + earlier)

    rank = jnp.zeros(destination.shape, f32)
    if tiles <= 16:
        for tile in range(tiles):
            rank = rank_of(tile, rank)
    else:
        rank = lax.fori_loop(0, tiles, rank_of, rank)
    rank = rank.astype(jnp.int32)
    slots[0] = (destination >> 1) * blocks + (rank >> 7)
    slots[1] = (destination & 1) * LANES + (rank & (LANES - 1))
    kind = source[...]
    factor = jnp.where(kind == 0, gain[0], jnp.where(kind == 1, gain[1], gain[2]))
    scaled = weight[...] * factor
    moment = scaled * value[...]
    pieces[0], pieces[1] = two_pieces(scaled)
    pieces[2], pieces[3] = two_pieces(moment)
    column = cell_col[...]
    pieces[4] = (cell_row[...] * 4 + (column >> 9)).astype(f32)
    pieces[5] = ((column & 511) - 256).astype(f32)

    slot_rows = row_count * blocks
    slot_ids = lax.broadcasted_iota(jnp.int32, (slot_rows, LANES), 0)
    lane_ids = lax.broadcasted_iota(jnp.int32, (2 * LANES, LANES), 0)
    routed[...] = jnp.zeros(routed.shape, f32)

    def place(step, carry):
        for r in range(8):
            here = pl.ds(step * 8 + r, 1)
            lanes = slice(r * LANES, (r + 1) * LANES)
            chosen = slot_ids == slots[0, here, :]
            left_route[:, lanes] = jnp.concatenate(
                [jnp.where(chosen, pieces[p, here, :], 0.0) for p in range(6)], axis=0
            ).astype(bf16)
            right_route[:, lanes] = jnp.where(
                lane_ids == slots[1, here, :], 1.0, 0.0
            ).astype(bf16)
        routed[...] += lax.dot_general(
            left_route[...], right_route[...], NT, preferred_element_type=f32
        )
        return carry

    lax.fori_loop(0, sounding_rows // 8, place, 0)

    def piece(p):
        return routed[p * slot_rows : (p + 1) * slot_rows, :]

    packed = piece(4)
    placed_row = jnp.floor(packed * 0.25)
    placed_col = (packed - 4.0 * placed_row) * 512.0 + (piece(5) + 256.0)
    values = (piece(0) + piece(1), piece(2) + piece(3), placed_row, placed_col)
    for v in range(4):
        for r in range(row_count):
            for c in range(2):
                outbox[2 * r + c, v * blocks : (v + 1) * blocks, :] = values[v][
                    r * blocks : (r + 1) * blocks, c * LANES : (c + 1) * LANES
                ]

    pl.semaphore_wait(barrier, tiles - 1)

    def sounding_copy(peer):
        return pltpu.make_async_remote_copy(
            src_ref=outbox.at[peer], dst_ref=inbox.at[me],
            send_sem=send_sem.at[peer], recv_sem=recv_sem.at[me],
            device_id={"row": peer // 2, "col": lax.rem(peer, 2)}, device_id_type=MESH,
        )

    def arrived(origin):
        pltpu.make_async_remote_copy(
            src_ref=outbox.at[origin], dst_ref=inbox.at[origin],
            send_sem=send_sem.at[origin], recv_sem=recv_sem.at[origin],
            device_id={"row": origin // 2, "col": lax.rem(origin, 2)}, device_id_type=MESH,
        ).wait_recv()

    sounding_copy(2 * my_row + other).start()

    def send(step, carry):
        peer_row = lax.rem(my_row + row_count - step, row_count)
        sounding_copy(2 * peer_row + my_col).start()
        sounding_copy(2 * peer_row + other).start()
        return carry

    lax.fori_loop(1, row_count, send, 0)

    strip = pl.ds(pl.multiple_of((1 - my_col) * (tile_cols - LANES), LANES), LANES)
    side = pl.ds(tile_cols, LANES)
    body = pl.ds(0, tile_cols)
    top, bottom = pl.ds(MARGIN, HALO), pl.ds(MARGIN + HALO + tile_rows, HALO)
    has_up, has_down = my_row > 0, my_row < row_count - 1

    def halo_copies(cut, put, sends, recvs):
        first, last = (0, HALO), (tile_rows - HALO, HALO)
        plan = (
            (has_up, -1, my_col, first, body, bottom, body),
            (has_down, 1, my_col, last, body, top, body),
            (None, 0, other, (0, tile_rows), strip, interior, side),
            (has_up, -1, other, first, strip, bottom, side),
            (has_down, 1, other, last, strip, top, side),
        )
        return [
            (
                condition,
                pltpu.make_async_remote_copy(
                    src_ref=cut(rows, columns), dst_ref=put(to_rows, to_columns),
                    send_sem=sends.at[n], recv_sem=recvs.at[n],
                    device_id={
                        "row": jnp.clip(my_row + shift, 0, row_count - 1),
                        "col": to_col,
                    },
                    device_id_type=MESH,
                ),
            )
            for n, (condition, shift, to_col, rows, columns, to_rows, to_columns) in enumerate(plan)
        ]

    def under(condition, action):
        if condition is None:
            action()
        else:
            pl.when(condition)(action)

    mirrored = (has_down, has_up, None, has_down, has_up)

    def finish(copies, which=range(5)):
        for (condition, copy), n in zip(copies, which):
            from_there = mirrored[n]
            under(condition, copy.wait_send)
            under(from_there, copy.wait_recv)

    field_copies = halo_copies(
        lambda rows, columns: start.at[pl.ds(*rows), columns],
        lambda rows, columns: field.at[0, rows, columns],
        halo_send, halo_recv,
    )
    for condition, copy in field_copies:
        under(condition, copy.start)

    def blank(rows):
        def action():
            field[0, rows, :] = jnp.zeros((HALO, field.shape[2]), f32)
            grid[:, rows, :] = jnp.zeros((2, HALO, field.shape[2]), f32)
        return action

    pl.when(jnp.logical_not(has_up))(blank(top))
    pl.when(jnp.logical_not(has_down))(blank(bottom))
    for n in range(SWEEPS):
        field[n, :MARGIN, :] = jnp.zeros((MARGIN, field.shape[2]), f32)
        field[n, MARGIN + ext_rows :, :] = jnp.zeros((MARGIN, field.shape[2]), f32)
    start_load.wait()

    row_ids = lax.broadcasted_iota(jnp.int32, (tile_rows, LANES), 0).astype(f32)
    col_ids = lax.broadcasted_iota(jnp.int32, (LANES, LANES), 0).astype(f32)
    chunks = tile_cols // LANES

    late = left.shape[0]
    span = tile_cols // PARTS
    span_chunks = span // LANES

    def prepare(source_row, slot):
        for c in range(2):
            origin = 2 * source_row + c
            for b in range(blocks):
                lanes = slice((c * blocks + b) * LANES, (c * blocks + b + 1) * LANES)
                w, m, r, k = (
                    inbox[origin, v * blocks + b : v * blocks + b + 1, :] for v in range(4)
                )
                (w_high, w_low), (m_high, m_low) = two_pieces(w), two_pieces(m)
                chosen = row_ids == r
                left[slot, :, lanes] = jnp.concatenate(
                    [jnp.where(chosen, x, 0.0) for x in (w_high, m_high, w_low, m_low)], axis=0
                ).astype(bf16)
                chunk = jnp.floor(k * (1.0 / LANES))
                base[slot, :, lanes] = jnp.where(
                    col_ids == k - LANES * chunk, 1.0, 0.0
                ).astype(bf16)
                chunk_of[slot, :, lanes] = jnp.broadcast_to(chunk, (8, LANES))

    def spread(target, slot, offset, first_chunk, count):
        for b in range(2 * blocks):
            lanes = slice(b * LANES, (b + 1) * LANES)
            to = slice(offset + b * LANES, offset + (b + 1) * LANES)
            shared = base[slot, :, lanes].reshape(LANES // 16, 16, LANES)
            chunk = chunk_of[slot, :, lanes]
            chunk = jnp.concatenate([chunk, chunk], axis=0)
            for n in range(count):
                mask = jnp.where(chunk == first_chunk + float(n), 1.0, 0.0).astype(bf16)
                target[n * LANES : (n + 1) * LANES, to] = (shared * mask[None]).reshape(
                    LANES, LANES
                )

    def grid_pair(source_row, begin):
        prepare(source_row, 0)
        spread(right, 0, 0, 0.0, chunks)
        term = lax.dot_general(right[...], left[0], NT, preferred_element_type=f32)
        if begin:
            total[...] = term
        else:
            total[...] += term

    inbox[me] = outbox[me]
    arrived(2 * my_row + other)
    grid_pair(my_row, True)

    def grid_step(step, carry):
        source_row = lax.rem(my_row + step, row_count)
        arrived(2 * source_row)
        arrived(2 * source_row + 1)
        grid_pair(source_row, False)
        return carry

    lax.fori_loop(1, row_count - late, grid_step, 0)

    def late_step(slot, carry):
        source_row = lax.rem(my_row + row_count - late + slot, row_count)
        arrived(2 * source_row)
        arrived(2 * source_row + 1)
        prepare(source_row, slot)
        return carry

    lax.fori_loop(0, late, late_step, 0)

    grid_copies = halo_copies(
        lambda rows, columns: grid.at[:, pl.ds(MARGIN + HALO + rows[0], rows[1]), columns],
        lambda rows, columns: grid.at[:, rows, columns],
        grid_send, grid_recv,
    )
    beside_copies = grid_copies[2:]

    def row_copies(part):
        columns = pl.ds(pl.multiple_of(part * span, LANES), span)
        plan = (
            (has_up, -1, pl.ds(MARGIN + HALO, HALO), bottom),
            (has_down, 1, pl.ds(MARGIN + tile_rows, HALO), top),
        )
        return [
            (
                condition,
                pltpu.make_async_remote_copy(
                    src_ref=grid.at[:, rows, columns], dst_ref=grid.at[:, to_rows, columns],
                    send_sem=row_send.at[n, part], recv_sem=row_recv.at[n, part],
                    device_id={
                        "row": jnp.clip(my_row + shift, 0, row_count - 1), "col": my_col
                    },
                    device_id_type=MESH,
                ),
            )
            for n, (condition, shift, rows, to_rows) in enumerate(plan)
        ]

    half = 2 * tile_rows
    depth = left.shape[2]

    def part_step(step, carry):
        part = step + (1 - my_col) * (PARTS - 1 - 2 * step)
        first_chunk = (part * span_chunks).astype(f32)
        term = total[pl.ds(pl.multiple_of(part * span, LANES), span), :]
        for slot in range(late):
            spread(right_late, slot, slot * depth, first_chunk, span_chunks)
        for slot in range(late):
            term = term + lax.dot_general(
                right_late[:, slot * depth : (slot + 1) * depth], left[slot], NT,
                preferred_element_type=f32,
            )
        for n in range(span_chunks):
            piece = term[n * LANES : (n + 1) * LANES]
            both = (piece[:, :half] + piece[:, half:]).T
            lanes = pl.ds(pl.multiple_of(part * span + n * LANES, LANES), LANES)
            scale = damping / (centre_weight + both[:tile_rows])
            grid[0, interior, lanes] = scale
            grid[1, interior, lanes] = scale * both[tile_rows:]

        @pl.when(step == 0)
        def _():
            for condition, copy in beside_copies:
                under(condition, copy.start)

        for condition, copy in row_copies(part):
            under(condition, copy.start)
        return carry

    lax.fori_loop(0, PARTS, part_step, 0)

    def sent(step, carry):
        peer = lax.rem(me + step, tiles)
        sounding_copy(peer).wait_send()
        return carry

    lax.fori_loop(1, tiles, sent, 0)
    finish(field_copies)
    grid_copies[2][1].wait()

    def keep_nearer(ref, rows, n):
        strip_lane = lax.broadcasted_iota(jnp.int32, (rows.stop - rows.start, LANES), 1)
        nearer = (strip_lane < LANES // 2) == (my_col == 0)
        ref[n, rows, tile_cols:] = jnp.where(nearer, ref[n, rows, tile_cols:], 0.0)

    first_row, last_row = MARGIN + HALO, MARGIN + HALO + tile_rows
    keep_nearer(field, slice(MARGIN, MARGIN + ext_rows), 0)
    for n in range(2):
        keep_nearer(grid, slice(first_row, last_row), n)

    width = field.shape[2]

    def relaxed(now, at):
        centre = field[now, at : at + 8, :]
        ring = field[now, at - 1 : at + 7, :] + field[now, at + 1 : at + 9, :]
        far = field[now, at - 2 : at + 6, :] + field[now, at + 2 : at + 10, :]
        beside = near_weight * centre - corner_weight * ring
        beside = pltpu.roll(beside, 1, 1) + pltpu.roll(beside, width - 1, 1)
        far = far + (pltpu.roll(centre, 2, 1) + pltpu.roll(centre, width - 2, 1))
        pull = near_weight * ring + beside - distant_weight * far
        return 0.5 * centre + (grid[1, at : at + 8, :] + grid[0, at : at + 8, :] * pull)

    def update(level, rows):
        for at in rows:
            field[level + 1, at : at + 8, :] = relaxed(level, at)

    def finished(rows):
        for at in rows:
            new = relaxed(SWEEPS - 1, at)
            out[at - first_row : at - first_row + 8, :] = new[:, :tile_cols]

    def inner(level, carry):
        update(level, range(first_row, last_row, 8))
        return carry

    lax.fori_loop(0, SWEEPS - 1, inner, 0)
    finished(range(first_row + 8, last_row - 8, 8))

    finish(beside_copies[1:], (3, 4))

    def rows_done(part, carry):
        finish(row_copies(part))
        return carry

    lax.fori_loop(0, PARTS, rows_done, 0)
    for rows in (slice(MARGIN, first_row), slice(last_row, last_row + HALO)):
        for n in range(2):
            keep_nearer(grid, rows, n)
    edges = (first_row - 8, last_row)
    ends = (first_row, last_row - 8)
    update(0, edges)

    def outer(level, carry):
        update(level, edges + ends)
        return carry

    lax.fori_loop(1, SWEEPS - 1, outer, 0)
    finished(ends)


def body(
    start, dest_tile, cell_row, cell_col, source_type, sounding_value, sounding_weight, type_gain
):
    tile_rows, tile_cols = start.shape
    row_count = lax.axis_size("row")
    assert lax.axis_size("col") == 2
    assert tile_rows == 64 and tile_cols <= 2048 and tile_cols % (PARTS * LANES) == 0
    count = dest_tile.shape[0]
    assert count % (8 * LANES) == 0
    sounding_rows = count // LANES
    tiles = 2 * row_count
    capacity = 5 * count // (4 * tiles)
    blocks = -(-capacity // LANES)
    box_rows = -(-4 * blocks // 8) * 8
    slot_rows = row_count * blocks
    width = tile_cols + LANES
    tall = tile_rows + 2 * HALO + 2 * MARGIN
    depth = 2 * blocks * LANES
    late = min(LATE, row_count // 2)
    vmem = pl.BlockSpec(memory_space=pltpu.VMEM)
    call = pl.pallas_call(
        functools.partial(kernel, row_count, blocks),
        out_shape=jax.ShapeDtypeStruct(start.shape, f32),
        in_specs=[pl.BlockSpec(memory_space=pltpu.HBM)] * 8,
        out_specs=vmem,
        scratch_shapes=[
            pltpu.VMEM((4, sounding_rows, LANES), jnp.int32),
            pltpu.VMEM((2, sounding_rows, LANES), f32),
            pltpu.SMEM((3,), f32),
            pltpu.SemaphoreType.DMA((8,)),
            pltpu.VMEM((tiles, box_rows, LANES), f32),
            pltpu.VMEM((tiles, box_rows, LANES), f32),
            pltpu.VMEM((6 * slot_rows, 8 * LANES), bf16),
            pltpu.VMEM((2 * LANES, 8 * LANES), bf16),
            pltpu.VMEM((6 * slot_rows, 2 * LANES), f32),
            pltpu.VMEM((2, sounding_rows, LANES), jnp.int32),
            pltpu.VMEM((6, sounding_rows, LANES), f32),
            pltpu.VMEM((late, 4 * tile_rows, depth), bf16),
            pltpu.VMEM((late, LANES, depth), bf16),
            pltpu.VMEM((late, 8, depth), f32),
            pltpu.VMEM((tile_cols, depth), bf16),
            pltpu.VMEM((tile_cols // PARTS, late * depth), bf16),
            pltpu.VMEM((tile_cols, 4 * tile_rows), f32),
            pltpu.VMEM((SWEEPS, tall, width), f32),
            pltpu.VMEM((2, tall, width), f32),
            pltpu.SemaphoreType.DMA((tiles,)),
            pltpu.SemaphoreType.DMA((tiles,)),
            pltpu.SemaphoreType.DMA((5,)),
            pltpu.SemaphoreType.DMA((5,)),
            pltpu.SemaphoreType.DMA((5,)),
            pltpu.SemaphoreType.DMA((5,)),
            pltpu.SemaphoreType.DMA((2, PARTS)),
            pltpu.SemaphoreType.DMA((2, PARTS)),
        ],
        compiler_params=pltpu.CompilerParams(
            collective_id=0, has_side_effects=True,
            vmem_limit_bytes=63 * 1024 * 1024
        ),
    )
    shaped = (sounding_rows, LANES)
    return call(
        start, dest_tile.reshape(shaped), cell_row.reshape(shaped), cell_col.reshape(shaped),
        source_type.reshape(shaped), sounding_value.reshape(shaped),
        sounding_weight.reshape(shaped), type_gain,
    )


def solution(mesh):
    many = P(("slab", "row", "col"))
    in_specs = (P(("slab", "row"), "col"), many, many, many, many, many, many, P())
    out_specs = P(("slab", "row"), "col")
    return jax.shard_map(body, mesh=mesh, in_specs=in_specs, out_specs=out_specs, check_vma=False)
```

```python
import functools

import jax
import jax.numpy as jnp
from jax import lax
from jax.experimental import pallas as pl
from jax.experimental.pallas import tpu as pltpu
from jax.sharding import PartitionSpec as P

SWEEPS = 4
PARTS = 4
LATE = 4
PLACED = 16
LANES = 128
HALO = 2 * SWEEPS
MARGIN = 8
MESH = pl.DeviceIdType.MESH

tension = 0.35
centre_weight = 20.0 * (1.0 - tension) + 4.0 * tension
near_weight = 8.0 * (1.0 - tension) + tension
corner_weight = 2.0 * (1.0 - tension)
distant_weight = 1.0 - tension
damping = 0.5

f32 = jnp.float32
bf16 = jnp.bfloat16
NT = (((1,), (1,)), ((), ()))


def two_pieces(x):
    high = x.astype(bf16).astype(f32)
    return high, x - high


def kernel(row_count, blocks, start, *refs):
    soundings, gain_in, out = refs[:6], refs[6], refs[7]
    whole_numbers, reals, gain, load_sem = refs[8:12]
    dest, cell_row, cell_col, source = (whole_numbers.at[n] for n in range(4))
    value, weight = (reals.at[n] for n in range(2))
    (
        outbox, inbox, left_route, right_route, routed, slots, pieces,
        left, base, chunk_of, right, right_late, total, field, grid, send_sem,
        recv_sem, halo_send, halo_recv, grid_send, grid_recv, row_send, row_recv,
    ) = refs[12:]
    tile_rows, tile_cols = start.shape
    sounding_rows = dest.shape[0]
    tiles = 2 * row_count
    my_row, my_col = lax.axis_index("row"), lax.axis_index("col")
    me = 2 * my_row + my_col
    other = 1 - my_col
    ext_rows = tile_rows + 2 * HALO
    interior = pl.ds(MARGIN + HALO, tile_rows)

    loads = [
        pltpu.make_async_copy(array, place, load_sem.at[n])
        for n, (array, place) in enumerate(
            zip(soundings, (dest, cell_row, cell_col, source, value, weight))
        )
    ]
    loads.append(pltpu.make_async_copy(gain_in, gain, load_sem.at[6]))
    start_load = pltpu.make_async_copy(
        start, field.at[0, interior, pl.ds(0, tile_cols)], load_sem.at[7]
    )
    for load in loads:
        load.start()
    start_load.start()

    barrier = pltpu.get_barrier_semaphore()

    def greet(step, carry):
        peer = lax.rem(me + step, tiles)
        pl.semaphore_signal(
            barrier, inc=1, device_id={"row": peer // 2, "col": lax.rem(peer, 2)},
            device_id_type=MESH,
        )
        return carry

    lax.fori_loop(1, tiles, greet, 0)

    loads[0].wait()
    destination = dest[...]
    lane_a = lax.broadcasted_iota(jnp.int32, (LANES, 2 * LANES), 0)
    lane_b = lax.broadcasted_iota(jnp.int32, (LANES, 2 * LANES), 1)
    before = jnp.where((lane_a < lane_b) | (lane_b >= LANES), 1.0, 0.0).astype(bf16)
    sub_a = lax.broadcasted_iota(jnp.int32, (sounding_rows, sounding_rows), 0)
    sub_b = lax.broadcasted_iota(jnp.int32, (sounding_rows, sounding_rows), 1)
    above = jnp.where(sub_b < sub_a, 1.0, 0.0).astype(bf16)

    def rank_of(tile, rank):
        hit = jnp.where(destination == tile, 1.0, 0.0)
        both = jnp.dot(hit.astype(bf16), before, preferred_element_type=f32)
        earlier = jnp.dot(
            above, both[:, LANES:].astype(bf16), preferred_element_type=f32
        )
        return rank + hit * (both[:, :LANES] + earlier)

    rank = jnp.zeros(destination.shape, f32)
    if tiles <= 16:
        for tile in range(tiles):
            rank = rank_of(tile, rank)
    else:
        rank = lax.fori_loop(0, tiles, rank_of, rank)
    rank = rank.astype(jnp.int32)
    slots[0] = (destination >> 1) * blocks + (rank >> 7)
    slots[1] = (destination & 1) * LANES + (rank & (LANES - 1))
    for load in loads[1:]:
        load.wait()
    kind = source[...]
    factor = jnp.where(kind == 0, gain[0], jnp.where(kind == 1, gain[1], gain[2]))
    scaled = weight[...] * factor
    moment = scaled * value[...]
    pieces[0], pieces[1] = two_pieces(scaled)
    pieces[2], pieces[3] = two_pieces(moment)
    column = cell_col[...]
    pieces[4] = (cell_row[...] * 4 + (column >> 9)).astype(f32)
    pieces[5] = ((column & 511) - 256).astype(f32)

    slot_rows = row_count * blocks
    slot_ids = lax.broadcasted_iota(jnp.int32, (slot_rows, LANES), 0)
    lane_ids = lax.broadcasted_iota(jnp.int32, (2 * LANES, LANES), 0)
    routed[...] = jnp.zeros(routed.shape, f32)

    def place(step, carry):
        for r in range(PLACED):
            here = pl.ds(step * PLACED + r, 1)
            lanes = slice(r * LANES, (r + 1) * LANES)
            chosen = slot_ids == slots[0, here, :]
            left_route[:, lanes] = jnp.concatenate(
                [jnp.where(chosen, pieces[p, here, :], 0.0) for p in range(6)], axis=0
            ).astype(bf16)
            right_route[:, lanes] = jnp.where(
                lane_ids == slots[1, here, :], 1.0, 0.0
            ).astype(bf16)
        routed[...] += lax.dot_general(
            left_route[...], right_route[...], NT, preferred_element_type=f32
        )
        return carry

    lax.fori_loop(0, sounding_rows // PLACED, place, 0)

    def piece(p):
        return routed[p * slot_rows : (p + 1) * slot_rows, :]

    packed = piece(4)
    placed_row = jnp.floor(packed * 0.25)
    placed_col = (packed - 4.0 * placed_row) * 512.0 + (piece(5) + 256.0)
    values = (piece(0) + piece(1), piece(2) + piece(3), placed_row, placed_col)
    for v in range(4):
        for r in range(row_count):
            for c in range(2):
                outbox[2 * r + c, v * blocks : (v + 1) * blocks, :] = values[v][
                    r * blocks : (r + 1) * blocks, c * LANES : (c + 1) * LANES
                ]

    pl.semaphore_wait(barrier, tiles - 1)

    def sounding_copy(peer):
        return pltpu.make_async_remote_copy(
            src_ref=outbox.at[peer], dst_ref=inbox.at[me],
            send_sem=send_sem.at[peer], recv_sem=recv_sem.at[me],
            device_id={"row": peer // 2, "col": lax.rem(peer, 2)}, device_id_type=MESH,
        )

    def arrived(origin):
        pltpu.make_async_remote_copy(
            src_ref=outbox.at[origin], dst_ref=inbox.at[origin],
            send_sem=send_sem.at[origin], recv_sem=recv_sem.at[origin],
            device_id={"row": origin // 2, "col": lax.rem(origin, 2)}, device_id_type=MESH,
        ).wait_recv()

    sounding_copy(2 * my_row + other).start()

    def send(step, carry):
        peer_row = lax.rem(my_row + row_count - step, row_count)
        sounding_copy(2 * peer_row + my_col).start()
        sounding_copy(2 * peer_row + other).start()
        return carry

    lax.fori_loop(1, row_count, send, 0)

    strip = pl.ds(pl.multiple_of((1 - my_col) * (tile_cols - LANES), LANES), LANES)
    side = pl.ds(tile_cols, LANES)
    body = pl.ds(0, tile_cols)
    top, bottom = pl.ds(MARGIN, HALO), pl.ds(MARGIN + HALO + tile_rows, HALO)
    has_up, has_down = my_row > 0, my_row < row_count - 1

    def halo_copies(cut, put, sends, recvs):
        first, last = (0, HALO), (tile_rows - HALO, HALO)
        plan = (
            (has_up, -1, my_col, first, body, bottom, body),
            (has_down, 1, my_col, last, body, top, body),
            (None, 0, other, (0, tile_rows), strip, interior, side),
            (has_up, -1, other, first, strip, bottom, side),
            (has_down, 1, other, last, strip, top, side),
        )
        return [
            (
                condition,
                pltpu.make_async_remote_copy(
                    src_ref=cut(rows, columns), dst_ref=put(to_rows, to_columns),
                    send_sem=sends.at[n], recv_sem=recvs.at[n],
                    device_id={
                        "row": jnp.clip(my_row + shift, 0, row_count - 1),
                        "col": to_col,
                    },
                    device_id_type=MESH,
                ),
            )
            for n, (condition, shift, to_col, rows, columns, to_rows, to_columns) in enumerate(plan)
        ]

    def under(condition, action):
        if condition is None:
            action()
        else:
            pl.when(condition)(action)

    mirrored = (has_down, has_up, None, has_down, has_up)

    def finish(copies, which=range(5)):
        for (condition, copy), n in zip(copies, which):
            from_there = mirrored[n]
            under(condition, copy.wait_send)
            under(from_there, copy.wait_recv)

    field_copies = halo_copies(
        lambda rows, columns: start.at[pl.ds(*rows), columns],
        lambda rows, columns: field.at[0, rows, columns],
        halo_send, halo_recv,
    )
    for condition, copy in field_copies:
        under(condition, copy.start)

    def blank(rows):
        def action():
            field[0, rows, :] = jnp.zeros((HALO, field.shape[2]), f32)
            grid[:, rows, :] = jnp.zeros((2, HALO, field.shape[2]), f32)
        return action

    pl.when(jnp.logical_not(has_up))(blank(top))
    pl.when(jnp.logical_not(has_down))(blank(bottom))
    for n in range(SWEEPS):
        field[n, :MARGIN, :] = jnp.zeros((MARGIN, field.shape[2]), f32)
        field[n, MARGIN + ext_rows :, :] = jnp.zeros((MARGIN, field.shape[2]), f32)
    start_load.wait()

    row_ids = lax.broadcasted_iota(jnp.int32, (tile_rows, LANES), 0).astype(f32)
    col_ids = lax.broadcasted_iota(jnp.int32, (LANES, LANES), 0).astype(f32)
    chunks = tile_cols // LANES

    late = left.shape[0]
    span = tile_cols // PARTS
    span_chunks = span // LANES

    def prepare(source_row, slot):
        for c in range(2):
            origin = 2 * source_row + c
            for b in range(blocks):
                lanes = slice((c * blocks + b) * LANES, (c * blocks + b + 1) * LANES)
                w, m, r, k = (
                    inbox[origin, v * blocks + b : v * blocks + b + 1, :] for v in range(4)
                )
                (w_high, w_low), (m_high, m_low) = two_pieces(w), two_pieces(m)
                chosen = row_ids == r
                left[slot, :, lanes] = jnp.concatenate(
                    [jnp.where(chosen, x, 0.0) for x in (w_high, m_high, w_low, m_low)], axis=0
                ).astype(bf16)
                chunk = jnp.floor(k * (1.0 / LANES))
                base[slot, :, lanes] = jnp.where(
                    col_ids == k - LANES * chunk, 1.0, 0.0
                ).astype(bf16)
                chunk_of[slot, :, lanes] = jnp.broadcast_to(chunk, (8, LANES))

    def spread(target, slot, offset, first_chunk, count):
        for b in range(2 * blocks):
            lanes = slice(b * LANES, (b + 1) * LANES)
            to = slice(offset + b * LANES, offset + (b + 1) * LANES)
            shared = base[slot, :, lanes].reshape(LANES // 16, 16, LANES)
            chunk = chunk_of[slot, :, lanes]
            chunk = jnp.concatenate([chunk, chunk], axis=0)
            for n in range(count):
                mask = jnp.where(chunk == first_chunk + float(n), 1.0, 0.0).astype(bf16)
                target[n * LANES : (n + 1) * LANES, to] = (shared * mask[None]).reshape(
                    LANES, LANES
                )

    def grid_pair(source_row, begin):
        prepare(source_row, 0)
        spread(right, 0, 0, 0.0, chunks)
        term = lax.dot_general(right[...], left[0], NT, preferred_element_type=f32)
        if begin:
            total[...] = term
        else:
            total[...] += term

    inbox[me] = outbox[me]
    arrived(2 * my_row + other)
    grid_pair(my_row, True)

    def grid_step(step, carry):
        source_row = lax.rem(my_row + step, row_count)
        arrived(2 * source_row)
        arrived(2 * source_row + 1)
        grid_pair(source_row, False)
        return carry

    lax.fori_loop(1, row_count - late, grid_step, 0)

    def late_step(slot, carry):
        source_row = lax.rem(my_row + row_count - late + slot, row_count)
        arrived(2 * source_row)
        arrived(2 * source_row + 1)
        prepare(source_row, slot)
        return carry

    lax.fori_loop(0, late, late_step, 0)

    grid_copies = halo_copies(
        lambda rows, columns: grid.at[:, pl.ds(MARGIN + HALO + rows[0], rows[1]), columns],
        lambda rows, columns: grid.at[:, rows, columns],
        grid_send, grid_recv,
    )
    beside_copies = grid_copies[2:]

    def row_copies(part):
        columns = pl.ds(pl.multiple_of(part * span, LANES), span)
        plan = (
            (has_up, -1, pl.ds(MARGIN + HALO, HALO), bottom),
            (has_down, 1, pl.ds(MARGIN + tile_rows, HALO), top),
        )
        return [
            (
                condition,
                pltpu.make_async_remote_copy(
                    src_ref=grid.at[:, rows, columns], dst_ref=grid.at[:, to_rows, columns],
                    send_sem=row_send.at[n, part], recv_sem=row_recv.at[n, part],
                    device_id={
                        "row": jnp.clip(my_row + shift, 0, row_count - 1), "col": my_col
                    },
                    device_id_type=MESH,
                ),
            )
            for n, (condition, shift, rows, to_rows) in enumerate(plan)
        ]

    half = 2 * tile_rows
    depth = left.shape[2]

    def part_step(step, carry):
        part = step + (1 - my_col) * (PARTS - 1 - 2 * step)
        first_chunk = (part * span_chunks).astype(f32)
        term = total[pl.ds(pl.multiple_of(part * span, LANES), span), :]
        for slot in range(late):
            spread(right_late, slot, slot * depth, first_chunk, span_chunks)
        for slot in range(late):
            term = term + lax.dot_general(
                right_late[:, slot * depth : (slot + 1) * depth], left[slot], NT,
                preferred_element_type=f32,
            )
        for n in range(span_chunks):
            piece = term[n * LANES : (n + 1) * LANES]
            both = (piece[:, :half] + piece[:, half:]).T
            lanes = pl.ds(pl.multiple_of(part * span + n * LANES, LANES), LANES)
            scale = damping / (centre_weight + both[:tile_rows])
            grid[0, interior, lanes] = scale
            grid[1, interior, lanes] = scale * both[tile_rows:]

        @pl.when(step == 0)
        def _():
            for condition, copy in beside_copies:
                under(condition, copy.start)

        for condition, copy in row_copies(part):
            under(condition, copy.start)
        return carry

    lax.fori_loop(0, PARTS, part_step, 0)

    def sent(step, carry):
        peer = lax.rem(me + step, tiles)
        sounding_copy(peer).wait_send()
        return carry

    lax.fori_loop(1, tiles, sent, 0)
    finish(field_copies)
    grid_copies[2][1].wait()

    def keep_nearer(ref, rows, n):
        strip_lane = lax.broadcasted_iota(jnp.int32, (rows.stop - rows.start, LANES), 1)
        nearer = (strip_lane < LANES // 2) == (my_col == 0)
        ref[n, rows, tile_cols:] = jnp.where(nearer, ref[n, rows, tile_cols:], 0.0)

    first_row, last_row = MARGIN + HALO, MARGIN + HALO + tile_rows
    keep_nearer(field, slice(MARGIN, MARGIN + ext_rows), 0)
    for n in range(2):
        keep_nearer(grid, slice(first_row, last_row), n)

    width = field.shape[2]

    def relaxed(now, at):
        centre = field[now, at : at + 8, :]
        ring = field[now, at - 1 : at + 7, :] + field[now, at + 1 : at + 9, :]
        far = field[now, at - 2 : at + 6, :] + field[now, at + 2 : at + 10, :]
        beside = near_weight * centre - corner_weight * ring
        beside = pltpu.roll(beside, 1, 1) + pltpu.roll(beside, width - 1, 1)
        far = far + (pltpu.roll(centre, 2, 1) + pltpu.roll(centre, width - 2, 1))
        pull = near_weight * ring + beside - distant_weight * far
        return 0.5 * centre + (grid[1, at : at + 8, :] + grid[0, at : at + 8, :] * pull)

    def update(level, rows):
        for at in rows:
            field[level + 1, at : at + 8, :] = relaxed(level, at)

    def finished(rows):
        for at in rows:
            new = relaxed(SWEEPS - 1, at)
            out[at - first_row : at - first_row + 8, :] = new[:, :tile_cols]

    def inner(level, carry):
        update(level, range(first_row, last_row, 8))
        return carry

    lax.fori_loop(0, SWEEPS - 1, inner, 0)
    finished(range(first_row + 8, last_row - 8, 8))

    finish(beside_copies[1:], (3, 4))

    def rows_done(part, carry):
        finish(row_copies(part))
        return carry

    lax.fori_loop(0, PARTS, rows_done, 0)
    for rows in (slice(MARGIN, first_row), slice(last_row, last_row + HALO)):
        for n in range(2):
            keep_nearer(grid, rows, n)
    edges = (first_row - 8, last_row)
    ends = (first_row, last_row - 8)
    update(0, edges)

    def outer(level, carry):
        update(level, edges + ends)
        return carry

    lax.fori_loop(1, SWEEPS - 1, outer, 0)
    finished(ends)


def body(
    start, dest_tile, cell_row, cell_col, source_type, sounding_value, sounding_weight, type_gain
):
    tile_rows, tile_cols = start.shape
    row_count = lax.axis_size("row")
    assert lax.axis_size("col") == 2
    assert tile_rows == 64 and tile_cols <= 2048 and tile_cols % (PARTS * LANES) == 0
    count = dest_tile.shape[0]
    assert count % (PLACED * LANES) == 0
    sounding_rows = count // LANES
    tiles = 2 * row_count
    capacity = 5 * count // (4 * tiles)
    blocks = -(-capacity // LANES)
    box_rows = -(-4 * blocks // 8) * 8
    slot_rows = row_count * blocks
    width = tile_cols + LANES
    tall = tile_rows + 2 * HALO + 2 * MARGIN
    depth = 2 * blocks * LANES
    late = min(LATE, row_count // 2)
    vmem = pl.BlockSpec(memory_space=pltpu.VMEM)
    call = pl.pallas_call(
        functools.partial(kernel, row_count, blocks),
        out_shape=jax.ShapeDtypeStruct(start.shape, f32),
        in_specs=[pl.BlockSpec(memory_space=pltpu.HBM)] * 8,
        out_specs=vmem,
        scratch_shapes=[
            pltpu.VMEM((4, sounding_rows, LANES), jnp.int32),
            pltpu.VMEM((2, sounding_rows, LANES), f32),
            pltpu.SMEM((3,), f32),
            pltpu.SemaphoreType.DMA((8,)),
            pltpu.VMEM((tiles, box_rows, LANES), f32),
            pltpu.VMEM((tiles, box_rows, LANES), f32),
            pltpu.VMEM((6 * slot_rows, PLACED * LANES), bf16),
            pltpu.VMEM((2 * LANES, PLACED * LANES), bf16),
            pltpu.VMEM((6 * slot_rows, 2 * LANES), f32),
            pltpu.VMEM((2, sounding_rows, LANES), jnp.int32),
            pltpu.VMEM((6, sounding_rows, LANES), f32),
            pltpu.VMEM((late, 4 * tile_rows, depth), bf16),
            pltpu.VMEM((late, LANES, depth), bf16),
            pltpu.VMEM((late, 8, depth), f32),
            pltpu.VMEM((tile_cols, depth), bf16),
            pltpu.VMEM((tile_cols // PARTS, late * depth), bf16),
            pltpu.VMEM((tile_cols, 4 * tile_rows), f32),
            pltpu.VMEM((SWEEPS, tall, width), f32),
            pltpu.VMEM((2, tall, width), f32),
            pltpu.SemaphoreType.DMA((tiles,)),
            pltpu.SemaphoreType.DMA((tiles,)),
            pltpu.SemaphoreType.DMA((5,)),
            pltpu.SemaphoreType.DMA((5,)),
            pltpu.SemaphoreType.DMA((5,)),
            pltpu.SemaphoreType.DMA((5,)),
            pltpu.SemaphoreType.DMA((2, PARTS)),
            pltpu.SemaphoreType.DMA((2, PARTS)),
        ],
        compiler_params=pltpu.CompilerParams(
            collective_id=0, has_side_effects=True,
            vmem_limit_bytes=63 * 1024 * 1024
        ),
    )
    shaped = (sounding_rows, LANES)
    return call(
        start, dest_tile.reshape(shaped), cell_row.reshape(shaped), cell_col.reshape(shaped),
        source_type.reshape(shaped), sounding_value.reshape(shaped),
        sounding_weight.reshape(shaped), type_gain,
    )


def solution(mesh):
    many = P(("slab", "row", "col"))
    in_specs = (P(("slab", "row"), "col"), many, many, many, many, many, many, P())
    out_specs = P(("slab", "row"), "col")
    return jax.shard_map(body, mesh=mesh, in_specs=in_specs, out_specs=out_specs, check_vma=False)
```
